32 devices in a mesh: wide: 16 (over z, y, core), narrow: 2 (over x).
Axes of the slice: x: 2, y: 2, z: 4, core: 2. Of those that a mesh axis runs over, the one named last changes fastest.
Arguments:
- vol_points: float32 [3, 32768], P(None, 'wide'), may hold values from 0 to 1
- vol_adjoint: bfloat16 [48, 32768], P(None, 'wide'), may hold values from -6 to 6
- surf_points: float32 [3, 4096], P(None, ('narrow', 'wide')), may hold values from 0 to 1
- tile_mask: int32 [256, 32], P('wide', 'narrow'), may hold values 0 or 1
Outputs:
- solution: float32 [48, 4096], P(None, ('narrow', 'wide'))
- residual: float32 [48, 4096], P(None, ('narrow', 'wide'))
The draws below stay inside these ranges and needn't reach their ends.
All inputs are finite; a program needn't handle non-finite values. No bound on the sum of `tile_mask` on one device may be relied on, other than what follows from the above.
Results may differ from the reference program's by a relative error of at most 0.0039.
Values sent between devices are 32-bit elements; how exact they have to be, the bound alone decides.
A program may use at most 64 MiB of HBM per device.

```python
import math
import jax
import jax.numpy as jnp
from jax import lax

OBJ_COLS = 48
TILE = 128
NV = 32768
NS = 4096


def place_ends(drawn, rng, smallest, largest):
    longest = drawn.shape.index(max(drawn.shape))
    spots = []
    for shift in (0, 1):
        where = [jax.random.randint(jax.random.fold_in(rng, axis), (), 0, length) for axis, length in enumerate(drawn.shape)]
        where[longest] = (where[longest] + shift) % drawn.shape[longest]
        spots.append(tuple(where))
    return drawn.at[spots[0]].set(smallest).at[spots[1]].set(largest)


def block_scale(own_key, dims, shards, low, largest):
    def one(dim, shards_of):
        steps = jax.random.uniform(jax.random.fold_in(jax.random.fold_in(own_key, 6), dim), (shards_of,), jnp.float32, low / len(shards), largest / len(shards))
        return jnp.repeat(jnp.exp(steps), dims[dim] // shards_of).reshape((-1,) + (1,) * (len(dims) - dim - 1))

    gain = one(*shards[0])
    for cut in shards[1:]:
        gain = gain * one(*cut)
    return gain


def scatter_about(key, shape, spread, limit, split=(), dtype=jnp.bfloat16):
    entries = jax.random.normal(key, shape, jnp.float32) * spread
    if len(split) > 0:
        entries = block_scale(key, shape, split, -0.22, 0.18) * entries
    return jnp.clip(entries, min=-limit, max=limit).astype(dtype)


def setup_inputs(seed: int = 0) -> dict:
    splits = jax.random.split(jax.random.key(seed), 5)
    return {
        "vol_points": jnp.clip(1.0 * jax.random.uniform(splits[0], (3, NV), jnp.float32) ** block_scale(splits[0], (3, NV), ((1, 16),), -0.2, 0.2), 0.0, 1.0),
        "vol_adjoint": scatter_about(splits[1], (OBJ_COLS, NV), 1.0, 6.0, ((1, 16),)),
        "surf_points": jnp.clip(1.0 * jax.random.uniform(splits[2], (3, NS), jnp.float32) ** block_scale(splits[2], (3, NS), ((1, 32),), -0.2, 0.2), 0.0, 1.0),
        "tile_mask": place_ends((jax.random.randint(splits[3], (NV // TILE, NS // TILE), 0, 4) < 3).astype(jnp.int32), jax.random.fold_in(splits[3], 1), 0, 1),
    }


RADIUS = 0.15
KERNEL_GAIN = 3200.0
RHS_GAIN = 28.0
LOWER_EDGE = 1.0
UPPER_EDGE = 4.0

def kernel_block(sources, targets):
    squared = jnp.zeros((sources.shape[1], targets.shape[1]), jnp.float32)
    for component in range(3):
        offset = sources[component][:, None] - targets[component][None, :]
        squared = squared + offset * offset
    scaled = jnp.sqrt(squared) / RADIUS
    remain = jnp.maximum(1.0 - scaled, 0.0)
    return remain ** 4 * (4.0 * scaled + 1.0)

def apply_operator(field, surf_points):
    width = math.gcd(NS, 512)

    def row_block(index):
        start = (index * width).astype(jnp.int32)
        targets = lax.dynamic_slice_in_dim(surf_points, start, width, 1)
        values = kernel_block(surf_points, targets)
        return jnp.dot(field, values, precision=lax.Precision.HIGHEST, preferred_element_type=jnp.float32)
    blocks = lax.map(row_block, jnp.arange(NS // width).astype(jnp.int32))
    mixed = jnp.transpose(blocks, (1, 0, 2)).reshape(field.shape[0], NS)
    return field + KERNEL_GAIN / NS * mixed

def reference(vol_points, vol_adjoint, surf_points, tile_mask):
    width = math.gcd(NS, 512)

    def column_block(index):
        start = (index * width).astype(jnp.int32)
        targets = lax.dynamic_slice_in_dim(surf_points, start, width, 1)
        mask_cols = lax.dynamic_slice_in_dim(tile_mask, (start // TILE).astype(jnp.int32), width // TILE, 1)
        expanded = jnp.repeat(jnp.repeat(mask_cols, TILE, 0), TILE, 1).astype(jnp.float32)
        values = (kernel_block(vol_points, targets) * expanded).astype(jnp.bfloat16)
        return jnp.dot(vol_adjoint, values, preferred_element_type=jnp.float32)
    blocks = lax.map(column_block, jnp.arange(NS // width).astype(jnp.int32))
    summed = jnp.transpose(blocks, (1, 0, 2)).reshape(vol_adjoint.shape[0], NS)
    rhs = summed * (RHS_GAIN / math.sqrt(NV))
    centre = (LOWER_EDGE + UPPER_EDGE) / 2.0
    half_width = (UPPER_EDGE - LOWER_EDGE) / 2.0
    sigma = centre / half_width
    rho_zero = 1.0 / sigma
    rho_one = 1.0 / (2.0 * sigma - rho_zero)
    first = rhs / centre
    near = rhs - apply_operator(first, surf_points)
    update = rho_one * rho_zero * first + 2.0 * rho_one / half_width * near
    solution = first + update
    residual = near - apply_operator(update, surf_points)
    return (solution, residual)
```

```python
import functools
import math

import jax
import jax.numpy as jnp
from jax import lax
from jax.experimental import pallas as pl
from jax.experimental.pallas import tpu as pltpu
from jax.sharding import PartitionSpec as P

TILE = 128
CHUNK = 256
RADIUS = 0.15
KERNEL_GAIN = 3200.0
RHS_GAIN = 28.0
LOWER_EDGE = 1.0
UPPER_EDGE = 4.0
SCALE = 4.0 / RADIUS
COORD_ROWS = 56
F32 = jnp.float32
BF16 = jnp.bfloat16
MESH = pl.DeviceIdType.MESH


def split3(x):
    high = x.astype(BF16).astype(F32)
    rest = x - high
    mid = rest.astype(BF16).astype(F32)
    return high, mid, rest - mid


def features(coords, left):
    row = lax.broadcasted_iota(jnp.int32, coords.shape, 0)
    p = jnp.where(row < 3, (coords - 0.5) * SCALE, 0.0)
    norm = jnp.sum(p * p, axis=0, keepdims=True)
    nh, nm, nl = split3(jnp.broadcast_to(norm, coords.shape))
    h, m, l = split3(p)
    one = jnp.where(row < 6, 1.0, 0.0)
    if left:
        h, m, l = -2.0 * h, -2.0 * m, -2.0 * l
        last = jnp.where(row == 3, nh, jnp.where(row == 4, nm, jnp.where(row == 5, nl, one)))
        groups = [h, h, m, m, h, l, last]
    else:
        last = jnp.where(row == 0, nh, jnp.where(row == 1, nm, jnp.where(row == 2, nl, one)))
        groups = [h, m, h, m, l, h, last]
    return jnp.concatenate(groups, axis=0)


def wendland(u):
    u = jnp.maximum(u, 1e-20)
    t = u * lax.rsqrt(u)
    r = jnp.maximum(4.0 - t, 0.0)
    r2 = r * r
    return r2 * r2 * (t + 1.0)


def kernel(dims, vol_ref, adj_ref, surf_ref, mask_ref, sol_ref, res_ref,
           own_xyz, xyz_z, xyz_r, vol_own, vol_in, mask_own, mask_in, vfeat, adjs,
           sfeat, rfeat, p_hi, p_lo, piece, rhs_in, field, field_in, part, part_in,
           sem_xs, sem_xz, sem_xr, sem_v, sem_ps, sem_pr, sem_fs, sem_fr, sem_ms, sem_mr):
    N, Z, Y, C, KP = dims
    R = N * Y * C
    ADJ, NVD = adj_ref.shape
    VT, ST = mask_ref.shape
    w = lax.axis_index("wide")
    n = lax.axis_index("narrow")
    z, y, c = w // (Y * C), (w // C) % Y, w % C
    me_r = (n * Y + y) * C + c
    me_z = z * Y + y

    def r_peer(d):
        pn = lax.rem(n + d // (Y * C), N)
        py = lax.rem(y + (d // C) % Y, Y)
        pc = lax.rem(c + d % C, C)
        return {"wide": (z * Y + py) * C + pc, "narrow": pn}, (pn * Y + py) * C + pc

    def z_peer(dz, dy):
        pz = lax.rem(z + dz, Z)
        py = lax.rem(y + dy, Y)
        return {"wide": (pz * Y + py) * C + c, "narrow": n}, pz, py

    def remote(src, dst, ssem, rsem, dev):
        return pltpu.make_async_remote_copy(
            src_ref=src, dst_ref=dst, send_sem=ssem, recv_sem=rsem,
            device_id=dev, device_id_type=MESH)

    zpairs = [(dz, dy) for dz in range(Z - 1, 0, -1) for dy in range(Y)]

    barrier = pltpu.get_barrier_semaphore()
    for d in range(1, R):
        pl.semaphore_signal(barrier, inc=1, device_id=r_peer(d)[0], device_id_type=MESH)
    for dz, dy in zpairs:
        pl.semaphore_signal(barrier, inc=1, device_id=z_peer(dz, dy)[0], device_id_type=MESH)

    own_xyz[...] = jnp.zeros_like(own_xyz)
    own_xyz[0:3, :] = surf_ref[...]
    vol_own[0:ADJ, :] = adj_ref[...].astype(F32)
    vol_own[ADJ:ADJ + 8, :] = jnp.zeros((8, NVD), F32)
    vol_own[ADJ:ADJ + 3, :] = vol_ref[...]
    mask_own[...] = jnp.zeros_like(mask_own)
    mask_own[:, 0:ST] = mask_ref[...].astype(F32)
    pl.semaphore_wait(barrier, R - 1 + len(zpairs))

    sends = []
    for k, (dz, dy) in enumerate(zpairs):
        dev, pz, py = z_peer(dz, dy)
        cp = remote(own_xyz, xyz_z.at[me_z], sem_xs.at[R + k], sem_xz.at[me_z], dev)
        cp.start()
        sends.append(cp)
    for d in range(1, R):
        dev, _ = r_peer(d)
        cp = remote(own_xyz, xyz_r.at[me_r], sem_xs.at[d], sem_xr.at[me_r], dev)
        cp.start()
        sends.append(cp)
    vsends = []
    if C > 1:
        dev, _ = r_peer(1)
        for k, (src, dst) in enumerate(((vol_own, vol_in), (mask_own, mask_in))):
            cp = remote(src, dst, sem_v.at[2 * k], sem_v.at[2 * k + 1], dev)
            cp.start()
            vsends.append(cp)

    expand = (lax.broadcasted_iota(jnp.int32, (VT, NVD), 1) // TILE
              == lax.broadcasted_iota(jnp.int32, (VT, NVD), 0)).astype(F32)

    def volume_features(s, vol, mask):
        adjs[s] = vol[0:ADJ, :].astype(BF16)
        f = features(vol[ADJ:ADJ + 8, :], False)
        m = lax.dot_general(mask[...], expand, (((0,), (0,)), ((), ())),
                            preferred_element_type=F32)
        pen = (1.0 - m) * 1024.0
        vfeat[s] = jnp.concatenate([f, pen[0:KP - COORD_ROWS, :]], axis=0).astype(BF16)

    volume_features(0, vol_own, mask_own)

    xyz_r[me_r] = own_xyz[...]
    for d in range(1, R):
        dev, s = r_peer(d)
        remote(own_xyz, xyz_r.at[s], sem_xs.at[d], sem_xr.at[s], dev).wait_recv()
    for dy in range(Y):
        py = lax.rem(y + dy, Y)
        xyz_z[z * Y + py] = xyz_r[(n * Y + py) * C + c]
    for k, (dz, dy) in enumerate(zpairs):
        dev, pz, py = z_peer(dz, dy)
        s = pz * Y + py
        remote(own_xyz, xyz_z.at[s], sem_xs.at[R + k], sem_xz.at[s], dev).wait_recv()

    extra = lax.broadcasted_iota(jnp.int32, (KP - COORD_ROWS, TILE), 0)
    for s in range(Z * Y):
        hot = jnp.where(extra == s * C + c, 1.0, 0.0)
        f = jnp.concatenate([features(xyz_z[s], True), hot], axis=0)
        sfeat[s] = f.T.astype(BF16)
    if C > 1:
        for cp in vsends:
            cp.wait_recv()
        volume_features(1, vol_in, mask_in)

    def surface_block(pz):
        left = sfeat[pl.ds(pz * Y, Y)].reshape(Y * TILE, KP)
        total = jnp.zeros((ADJ, Y * TILE), F32)
        for s in range(C):
            for k in range(0, NVD, CHUNK):
                u = jnp.dot(left, vfeat[s, :, k:k + CHUNK], preferred_element_type=F32)
                total = total + lax.dot_general(
                    adjs[s, :, k:k + CHUNK], wendland(u).astype(BF16),
                    (((1,), (1,)), ((), ())), preferred_element_type=F32)
        for q in range(Y):
            piece[pz * Y + q] = total[:, q * TILE:(q + 1) * TILE]

    def piece_copy(dz, dy):
        dev, pz, py = z_peer(dz, dy)
        s = pz * Y + py
        return remote(piece.at[s], rhs_in.at[me_z], sem_ps.at[s], sem_pr.at[me_z], dev)

    def piece_arrival(dz, dy):
        dev, pz, py = z_peer(dz, dy)
        s = pz * Y + py
        return remote(piece.at[s], rhs_in.at[s], sem_ps.at[s], sem_pr.at[s], dev), s

    def far(i, carry):
        dz = Z - 1 - i
        surface_block(lax.rem(z + dz, Z))
        for dy in range(Y):
            piece_copy(dz, dy).start()
        return carry

    lax.fori_loop(0, Z - 1, far, 0)
    surface_block(z)
    for dy in range(1, Y):
        piece_copy(0, dy).start()

    for s in range(R):
        f = jnp.concatenate(
            [features(xyz_r[s], False), jnp.zeros((KP - COORD_ROWS, TILE), F32)], axis=0)
        rfeat[:, s * TILE:(s + 1) * TILE] = f.astype(BF16)

    def kernel_rows(q, carry):
        left = sfeat[q * Y + y]
        for k in range(0, R * TILE, CHUNK):
            val = wendland(jnp.dot(left, rfeat[:, k:k + CHUNK], preferred_element_type=F32))
            high = val.astype(BF16)
            p_hi[q, :, k:k + CHUNK] = high
            p_lo[q, :, k:k + CHUNK] = (val - high.astype(F32)).astype(BF16)
        return carry

    lax.fori_loop(0, Z, kernel_rows, 0)

    rhs = piece[me_z]
    order = [(0, dy) for dy in range(1, Y)] + zpairs
    for dz, dy in order:
        cp, s = piece_arrival(dz, dy)
        cp.wait_recv()
        rhs = rhs + rhs_in[s]

    total_volume = NVD * Z * Y * C
    total_surface = TILE * Z * Y * C * N
    rhs = rhs * (RHS_GAIN / math.sqrt(total_volume) / 256.0)

    def apply_operator(o, value):
        field[o] = value
        out = []
        for dz in range(1, Z):
            dev, pz, _ = z_peer(dz, 0)
            cp = remote(field.at[o], field_in.at[o, z], sem_fs.at[o, dz], sem_fr.at[o, z], dev)
            cp.start()
            out.append(cp)

        def product(f, q):
            high = f.astype(BF16)
            low = (f - high.astype(F32)).astype(BF16)
            both = jnp.dot(jnp.concatenate([high, low], axis=0), p_hi[q],
                           preferred_element_type=F32)
            return (both[0:ADJ] + both[ADJ:]
                    + jnp.dot(high, p_lo[q], preferred_element_type=F32))

        total = product(value, z)
        for dz in range(1, Z):
            dev, pz, _ = z_peer(dz, 0)
            remote(field.at[o], field_in.at[o, pz], sem_fs.at[o, dz], sem_fr.at[o, pz],
                   dev).wait_recv()
            total = total + product(field_in[o, pz], pz)
        for s in range(R):
            part[o, s] = total[:, s * TILE:(s + 1) * TILE]
        for d in range(R - 1, 0, -1):
            dev, s = r_peer(d)
            cp = remote(part.at[o, s], part_in.at[o, me_r], sem_ms.at[o, d], sem_mr.at[o, me_r],
                        dev)
            cp.start()
            out.append(cp)
        mixed = part[o, me_r]
        for d in range(1, R):
            dev, s = r_peer(d)
            remote(part.at[o, s], part_in.at[o, s], sem_ms.at[o, d], sem_mr.at[o, s],
                   dev).wait_recv()
            mixed = mixed + part_in[o, s]
        return value + (KERNEL_GAIN / total_surface / 256.0) * mixed, out

    centre = (LOWER_EDGE + UPPER_EDGE) / 2.0
    half_width = (UPPER_EDGE - LOWER_EDGE) / 2.0
    sigma = centre / half_width
    rho_zero = 1.0 / sigma
    rho_one = 1.0 / (2.0 * sigma - rho_zero)
    first = rhs / centre
    mixed, out = apply_operator(0, first)
    sends += out
    near = rhs - mixed
    update = rho_one * rho_zero * first + (2.0 * rho_one / half_width) * near
    sol_ref[...] = first + update
    mixed, out = apply_operator(1, update)
    sends += out
    res_ref[...] = near - mixed

    for cp in sends + vsends:
        cp.wait_send()
    for dz, dy in order:
        piece_copy(dz, dy).wait_send()


def body(dims, vol_points, vol_adjoint, surf_points, tile_mask):
    N, Z, Y, C, KP = dims
    R = N * Y * C
    adj, nvd = vol_adjoint.shape
    vt = tile_mask.shape[0]
    vmem = pl.BlockSpec(memory_space=pltpu.VMEM)
    out = jax.ShapeDtypeStruct((adj, TILE), F32)
    lanes = -(-tile_mask.shape[1] // 128) * 128
    dma = pltpu.SemaphoreType.DMA
    return pl.pallas_call(
        functools.partial(kernel, dims),
        out_shape=(out, out),
        in_specs=[vmem] * 4,
        out_specs=(vmem, vmem),
        scratch_shapes=[
            pltpu.VMEM((8, TILE), F32),
            pltpu.VMEM((Z * Y, 8, TILE), F32),
            pltpu.VMEM((R, 8, TILE), F32),
            pltpu.VMEM((adj + 8, nvd), F32),
            pltpu.VMEM((adj + 8, nvd), F32),
            pltpu.VMEM((vt, lanes), F32),
            pltpu.VMEM((vt, lanes), F32),
            pltpu.VMEM((C, KP, nvd), BF16),
            pltpu.VMEM((C, adj, nvd), BF16),
            pltpu.VMEM((Z * Y, TILE, KP), BF16),
            pltpu.VMEM((KP, R * TILE), BF16),
            pltpu.VMEM((Z, TILE, R * TILE), BF16),
            pltpu.VMEM((Z, TILE, R * TILE), BF16),
            pltpu.VMEM((Z * Y, adj, TILE), F32),
            pltpu.VMEM((Z * Y, adj, TILE), F32),
            pltpu.VMEM((2, adj, TILE), F32),
            pltpu.VMEM((2, Z, adj, TILE), F32),
            pltpu.VMEM((2, R, adj, TILE), F32),
            pltpu.VMEM((2, R, adj, TILE), F32),
            dma((R + Z * Y,)),
            dma((Z * Y,)),
            dma((R,)),
            dma((4,)),
            dma((Z * Y,)),
            dma((Z * Y,)),
            dma((2, Z)),
            dma((2, Z)),
            dma((2, R)),
            dma((2, R)),
        ],
        compiler_params=pltpu.CompilerParams(
            collective_id=0, has_side_effects=True, vmem_limit_bytes=56 * 1024 * 1024),
    )(vol_points, vol_adjoint, surf_points, tile_mask)


def solution(mesh):
    wide, narrow = mesh.shape["wide"], mesh.shape["narrow"]
    core = math.gcd(wide, 2)
    rows = math.gcd(wide // core, 2)
    depth = -(-(COORD_ROWS + wide) // 128) * 128
    dims = (narrow, wide // core // rows, rows, core, depth)
    return jax.shard_map(
        functools.partial(body, dims),
        mesh=mesh,
        in_specs=(
            P(None, "wide"),
            P(None, "wide"),
            P(None, ("narrow", "wide")),
            P("wide", "narrow"),
        ),
        out_specs=(P(None, ("narrow", "wide")), P(None, ("narrow", "wide"))),
        check_vma=False,
    )
```

```python
import functools
import math

import jax
import jax.numpy as jnp
from jax import lax
from jax.experimental import pallas as pl
from jax.experimental.pallas import tpu as pltpu
from jax.sharding import PartitionSpec as P

TILE = 128
CHUNK = 256
RADIUS = 0.15
KERNEL_GAIN = 3200.0
RHS_GAIN = 28.0
LOWER_EDGE = 1.0
UPPER_EDGE = 4.0
SCALE = 4.0 / RADIUS
COORD_ROWS = 56
F32 = jnp.float32
BF16 = jnp.bfloat16
MESH = pl.DeviceIdType.MESH


def split3(x):
    high = x.astype(BF16).astype(F32)
    rest = x - high
    mid = rest.astype(BF16).astype(F32)
    return high, mid, rest - mid


def features(coords, left):
    row = lax.broadcasted_iota(jnp.int32, coords.shape, 0)
    p = jnp.where(row < 3, (coords - 0.5) * SCALE, 0.0)
    norm = jnp.sum(p * p, axis=0, keepdims=True)
    nh, nm, nl = split3(jnp.broadcast_to(norm, coords.shape))
    h, m, l = split3(p)
    one = jnp.where(row < 6, 1.0, 0.0)
    if left:
        h, m, l = -2.0 * h, -2.0 * m, -2.0 * l
        last = jnp.where(row == 3, nh, jnp.where(row == 4, nm, jnp.where(row == 5, nl, one)))
        groups = [h, h, m, m, h, l, last]
    else:
        last = jnp.where(row == 0, nh, jnp.where(row == 1, nm, jnp.where(row == 2, nl, one)))
        groups = [h, m, h, m, l, h, last]
    return jnp.concatenate(groups, axis=0)


def wendland(u):
    u = jnp.maximum(u, 1e-20)
    t = u * lax.rsqrt(u)
    r = jnp.maximum(4.0 - t, 0.0)
    r2 = r * r
    return r2 * r2 * (t + 1.0)


def kernel(dims, vol_hbm, adj_hbm, surf_hbm, mask_hbm, both_ref,
           vol_ref, adj_ref, surf_ref, mask_ref, sem_in,
           own_xyz, xyz_z, xyz_r, vol_own, vol_in, mask_own, mask_in, vfeat, adjs,
           sfeat, rfeat, p_hi, p_lo, piece, rhs_in, field, field_in, part, part_in,
           sem_xs, sem_xz, sem_xr, sem_v, sem_ps, sem_pr, sem_fs, sem_fr, sem_ms, sem_mr):
    N, Z, Y, C, KP = dims
    R = N * Y * C
    ADJ, NVD = adj_ref.shape
    VT, ST = mask_ref.shape
    w = lax.axis_index("wide")
    n = lax.axis_index("narrow")
    z, y, c = w // (Y * C), (w // C) % Y, w % C
    me_r = (n * Y + y) * C + c
    me_z = z * Y + y

    def r_peer(d):
        pn = lax.rem(n + d // (Y * C), N)
        py = lax.rem(y + (d // C) % Y, Y)
        pc = lax.rem(c + d % C, C)
        return {"wide": (z * Y + py) * C + pc, "narrow": pn}, (pn * Y + py) * C + pc

    def z_peer(dz, dy):
        pz = lax.rem(z + dz, Z)
        py = lax.rem(y + dy, Y)
        return {"wide": (pz * Y + py) * C + c, "narrow": n}, pz, py

    def remote(src, dst, ssem, rsem, dev):
        return pltpu.make_async_remote_copy(
            src_ref=src, dst_ref=dst, send_sem=ssem, recv_sem=rsem,
            device_id=dev, device_id_type=MESH)

    zpairs = [(dz, dy) for dz in range(Z - 1, 0, -1) for dy in range(Y)]

    loads = [pltpu.make_async_copy(src, dst, sem_in.at[k]) for k, (src, dst) in enumerate(
        ((surf_hbm, surf_ref), (mask_hbm, mask_ref), (vol_hbm, vol_ref), (adj_hbm, adj_ref)))]
    for cp in loads:
        cp.start()

    barrier = pltpu.get_barrier_semaphore()
    for d in range(1, R):
        pl.semaphore_signal(barrier, inc=1, device_id=r_peer(d)[0], device_id_type=MESH)
    for dz, dy in zpairs:
        pl.semaphore_signal(barrier, inc=1, device_id=z_peer(dz, dy)[0], device_id_type=MESH)

    for cp in loads:
        cp.wait()
    own_xyz[...] = jnp.zeros_like(own_xyz)
    own_xyz[0:3, :] = surf_ref[...]
    vol_own[0:ADJ, :] = adj_ref[...].astype(F32)
    vol_own[ADJ:ADJ + 8, :] = jnp.zeros((8, NVD), F32)
    vol_own[ADJ:ADJ + 3, :] = vol_ref[...]
    mask_own[...] = jnp.zeros_like(mask_own)
    mask_own[:, 0:ST] = mask_ref[...].astype(F32)
    pl.semaphore_wait(barrier, R - 1 + len(zpairs))

    sends = []
    for k, (dz, dy) in enumerate(zpairs):
        dev, pz, py = z_peer(dz, dy)
        cp = remote(own_xyz, xyz_z.at[me_z], sem_xs.at[R + k], sem_xz.at[me_z], dev)
        cp.start()
        sends.append(cp)
    for d in range(1, R):
        dev, _ = r_peer(d)
        cp = remote(own_xyz, xyz_r.at[me_r], sem_xs.at[d], sem_xr.at[me_r], dev)
        cp.start()
        sends.append(cp)
    vsends = []
    if C > 1:
        dev, _ = r_peer(1)
        for k, (src, dst) in enumerate(((vol_own, vol_in), (mask_own, mask_in))):
            cp = remote(src, dst, sem_v.at[2 * k], sem_v.at[2 * k + 1], dev)
            cp.start()
            vsends.append(cp)

    expand = (lax.broadcasted_iota(jnp.int32, (VT, NVD), 1) // TILE
              == lax.broadcasted_iota(jnp.int32, (VT, NVD), 0)).astype(F32)

    def volume_features(s, vol, mask):
        adjs[s] = vol[0:ADJ, :].astype(BF16)
        f = features(vol[ADJ:ADJ + 8, :], False)
        m = lax.dot_general(mask[...], expand, (((0,), (0,)), ((), ())),
                            preferred_element_type=F32)
        pen = (1.0 - m) * 1024.0
        vfeat[s] = jnp.concatenate([f, pen[0:KP - COORD_ROWS, :]], axis=0).astype(BF16)

    volume_features(0, vol_own, mask_own)

    xyz_r[me_r] = own_xyz[...]
    for d in range(1, R):
        dev, s = r_peer(d)
        remote(own_xyz, xyz_r.at[s], sem_xs.at[d], sem_xr.at[s], dev).wait_recv()
    for dy in range(Y):
        py = lax.rem(y + dy, Y)
        xyz_z[z * Y + py] = xyz_r[(n * Y + py) * C + c]
    for k, (dz, dy) in enumerate(zpairs):
        dev, pz, py = z_peer(dz, dy)
        s = pz * Y + py
        remote(own_xyz, xyz_z.at[s], sem_xs.at[R + k], sem_xz.at[s], dev).wait_recv()

    extra = lax.broadcasted_iota(jnp.int32, (KP - COORD_ROWS, TILE), 0)
    for s in range(Z * Y):
        hot = jnp.where(extra == s * C + c, 1.0, 0.0)
        f = jnp.concatenate([features(xyz_z[s], True), hot], axis=0)
        sfeat[s] = f.T.astype(BF16)
    if C > 1:
        for cp in vsends:
            cp.wait_recv()
        volume_features(1, vol_in, mask_in)

    def surface_block(pz):
        left = sfeat[pl.ds(pz * Y, Y)].reshape(Y * TILE, KP)
        total = jnp.zeros((ADJ, Y * TILE), F32)
        for s in range(C):
            for k in range(0, NVD, CHUNK):
                u = jnp.dot(left, vfeat[s, :, k:k + CHUNK], preferred_element_type=F32)
                total = total + lax.dot_general(
                    adjs[s, :, k:k + CHUNK], wendland(u).astype(BF16),
                    (((1,), (1,)), ((), ())), preferred_element_type=F32)
        for q in range(Y):
            piece[pz * Y + q] = total[:, q * TILE:(q + 1) * TILE]

    def piece_copy(dz, dy):
        dev, pz, py = z_peer(dz, dy)
        s = pz * Y + py
        return remote(piece.at[s], rhs_in.at[me_z], sem_ps.at[s], sem_pr.at[me_z], dev)

    def piece_arrival(dz, dy):
        dev, pz, py = z_peer(dz, dy)
        s = pz * Y + py
        return remote(piece.at[s], rhs_in.at[s], sem_ps.at[s], sem_pr.at[s], dev), s

    def far(i, carry):
        dz = Z - 1 - i
        surface_block(lax.rem(z + dz, Z))
        for dy in range(Y):
            piece_copy(dz, dy).start()
        return carry

    lax.fori_loop(0, Z - 1, far, 0)
    surface_block(z)
    for dy in range(1, Y):
        piece_copy(0, dy).start()

    for s in range(R):
        f = jnp.concatenate(
            [features(xyz_r[s], False), jnp.zeros((KP - COORD_ROWS, TILE), F32)], axis=0)
        rfeat[:, s * TILE:(s + 1) * TILE] = f.astype(BF16)

    def kernel_rows(q, carry):
        left = sfeat[q * Y + y]
        for k in range(0, R * TILE, CHUNK):
            val = wendland(jnp.dot(left, rfeat[:, k:k + CHUNK], preferred_element_type=F32))
            high = val.astype(BF16)
            p_hi[q, :, k:k + CHUNK] = high
            p_lo[q, :, k:k + CHUNK] = (val - high.astype(F32)).astype(BF16)
        return carry

    lax.fori_loop(0, Z, kernel_rows, 0)

    rhs = piece[me_z]
    order = [(0, dy) for dy in range(1, Y)] + zpairs
    for dz, dy in order:
        cp, s = piece_arrival(dz, dy)
        cp.wait_recv()
        rhs = rhs + rhs_in[s]

    total_volume = NVD * Z * Y * C
    total_surface = TILE * Z * Y * C * N
    rhs = rhs * (RHS_GAIN / math.sqrt(total_volume) / 256.0)

    def apply_operator(o, value):
        field[o] = value
        out = []
        for dz in range(1, Z):
            dev, pz, _ = z_peer(dz, 0)
            cp = remote(field.at[o], field_in.at[o, z], sem_fs.at[o, dz], sem_fr.at[o, z], dev)
            cp.start()
            out.append(cp)

        def product(f, q):
            high = f.astype(BF16)
            low = (f - high.astype(F32)).astype(BF16)
            both = jnp.dot(jnp.concatenate([high, low], axis=0), p_hi[q],
                           preferred_element_type=F32)
            return (both[0:ADJ] + both[ADJ:]
                    + jnp.dot(high, p_lo[q], preferred_element_type=F32))

        total = product(value, z)
        for dz in range(1, Z):
            dev, pz, _ = z_peer(dz, 0)
            remote(field.at[o], field_in.at[o, pz], sem_fs.at[o, dz], sem_fr.at[o, pz],
                   dev).wait_recv()
            total = total + product(field_in[o, pz], pz)
        for s in range(R):
            part[o, s] = total[:, s * TILE:(s + 1) * TILE]
        for d in range(R - 1, 0, -1):
            dev, s = r_peer(d)
            cp = remote(part.at[o, s], part_in.at[o, me_r], sem_ms.at[o, d], sem_mr.at[o, me_r],
                        dev)
            cp.start()
            out.append(cp)
        mixed = part[o, me_r]
        for d in range(1, R):
            dev, s = r_peer(d)
            remote(part.at[o, s], part_in.at[o, s], sem_ms.at[o, d], sem_mr.at[o, s],
                   dev).wait_recv()
            mixed = mixed + part_in[o, s]
        return value + (KERNEL_GAIN / total_surface / 256.0) * mixed, out

    centre = (LOWER_EDGE + UPPER_EDGE) / 2.0
    half_width = (UPPER_EDGE - LOWER_EDGE) / 2.0
    sigma = centre / half_width
    rho_zero = 1.0 / sigma
    rho_one = 1.0 / (2.0 * sigma - rho_zero)
    first = rhs / centre
    mixed, out = apply_operator(0, first)
    sends += out
    near = rhs - mixed
    update = rho_one * rho_zero * first + (2.0 * rho_one / half_width) * near
    both_ref[0] = first + update
    mixed, out = apply_operator(1, update)
    sends += out
    both_ref[1] = near - mixed

    for cp in sends + vsends:
        cp.wait_send()
    for dz, dy in order:
        piece_copy(dz, dy).wait_send()


def body(dims, vol_points, vol_adjoint, surf_points, tile_mask):
    N, Z, Y, C, KP = dims
    R = N * Y * C
    adj, nvd = vol_adjoint.shape
    vt = tile_mask.shape[0]
    vmem = pl.BlockSpec(memory_space=pltpu.VMEM)
    out = jax.ShapeDtypeStruct((2, adj, TILE), F32)
    lanes = -(-tile_mask.shape[1] // 128) * 128
    dma = pltpu.SemaphoreType.DMA
    both = pl.pallas_call(
        functools.partial(kernel, dims),
        out_shape=out,
        in_specs=[pl.BlockSpec(memory_space=pl.ANY)] * 4,
        out_specs=vmem,
        scratch_shapes=[
            pltpu.VMEM(vol_points.shape, F32),
            pltpu.VMEM(vol_adjoint.shape, BF16),
            pltpu.VMEM(surf_points.shape, F32),
            pltpu.VMEM(tile_mask.shape, jnp.int32),
            dma((4,)),
            pltpu.VMEM((8, TILE), F32),
            pltpu.VMEM((Z * Y, 8, TILE), F32),
            pltpu.VMEM((R, 8, TILE), F32),
            pltpu.VMEM((adj + 8, nvd), F32),
            pltpu.VMEM((adj + 8, nvd), F32),
            pltpu.VMEM((vt, lanes), F32),
            pltpu.VMEM((vt, lanes), F32),
            pltpu.VMEM((C, KP, nvd), BF16),
            pltpu.VMEM((C, adj, nvd), BF16),
            pltpu.VMEM((Z * Y, TILE, KP), BF16),
            pltpu.VMEM((KP, R * TILE), BF16),
            pltpu.VMEM((Z, TILE, R * TILE), BF16),
            pltpu.VMEM((Z, TILE, R * TILE), BF16),
            pltpu.VMEM((Z * Y, adj, TILE), F32),
            pltpu.VMEM((Z * Y, adj, TILE), F32),
            pltpu.VMEM((2, adj, TILE), F32),
            pltpu.VMEM((2, Z, adj, TILE), F32),
            pltpu.VMEM((2, R, adj, TILE), F32),
            pltpu.VMEM((2, R, adj, TILE), F32),
            dma((R + Z * Y,)),
            dma((Z * Y,)),
            dma((R,)),
            dma((4,)),
            dma((Z * Y,)),
            dma((Z * Y,)),
            dma((2, Z)),
            dma((2, Z)),
            dma((2, R)),
            dma((2, R)),
        ],
        compiler_params=pltpu.CompilerParams(
            collective_id=0, has_side_effects=True, vmem_limit_bytes=56 * 1024 * 1024),
    )(vol_points, vol_adjoint, surf_points, tile_mask)
    return both[0], both[1]


def solution(mesh):
    wide, narrow = mesh.shape["wide"], mesh.shape["narrow"]
    core = math.gcd(wide, 2)
    rows = math.gcd(wide // core, 2)
    depth = -(-(COORD_ROWS + wide) // 128) * 128
    dims = (narrow, wide // core // rows, rows, core, depth)
    return jax.shard_map(
        functools.partial(body, dims),
        mesh=mesh,
        in_specs=(
            P(None, "wide"),
            P(None, "wide"),
            P(None, ("narrow", "wide")),
            P("wide", "narrow"),
        ),
        out_specs=(P(None, ("narrow", "wide")), P(None, ("narrow", "wide"))),
        check_vma=False,
    )
```

```python
import functools
import math

import jax
import jax.numpy as jnp
from jax import lax
from jax.experimental import pallas as pl
from jax.experimental.pallas import tpu as pltpu
from jax.sharding import PartitionSpec as P

TILE = 128
CHUNK = 256
RADIUS = 0.15
KERNEL_GAIN = 3200.0
RHS_GAIN = 28.0
LOWER_EDGE = 1.0
UPPER_EDGE = 4.0
SCALE = 4.0 / RADIUS
COORD_ROWS = 56
F32 = jnp.float32
BF16 = jnp.bfloat16
MESH = pl.DeviceIdType.MESH


def split3(x):
    high = x.astype(BF16).astype(F32)
    rest = x - high
    mid = rest.astype(BF16).astype(F32)
    return high, mid, rest - mid


def features(coords, left):
    row = lax.broadcasted_iota(jnp.int32, coords.shape, 0)
    p = jnp.where(row < 3, (coords - 0.5) * SCALE, 0.0)
    norm = jnp.sum(p * p, axis=0, keepdims=True)
    nh, nm, nl = split3(jnp.broadcast_to(norm, coords.shape))
    h, m, l = split3(p)
    one = jnp.where(row < 6, 1.0, 0.0)
    if left:
        h, m, l = -2.0 * h, -2.0 * m, -2.0 * l
        last = jnp.where(row == 3, nh, jnp.where(row == 4, nm, jnp.where(row == 5, nl, one)))
        groups = [h, h, m, m, h, l, last]
    else:
        last = jnp.where(row == 0, nh, jnp.where(row == 1, nm, jnp.where(row == 2, nl, one)))
        groups = [h, m, h, m, l, h, last]
    return jnp.concatenate(groups, axis=0)


def wendland(u):
    u = jnp.maximum(u, 1e-20)
    t = u * lax.rsqrt(u)
    r = jnp.maximum(4.0 - t, 0.0)
    r2 = r * r
    return r2 * r2 * (t + 1.0)


def kernel(dims, vol_hbm, adj_hbm, surf_hbm, mask_hbm, both_ref,
           vol_ref, adj_ref, surf_ref, mask_ref, sem_in,
           own_xyz, xyz_z, xyz_r, vol_own, vol_in, mask_own, mask_in, vfeat, adjs,
           sfeat, rfeat, p_hi, p_lo, piece, rhs_in, field, field_in, part, part_in,
           sem_xs, sem_xz, sem_xr, sem_v, sem_ps, sem_pr, sem_fs, sem_fr, sem_ms, sem_mr):
    N, Z, Y, C, KP = dims
    R = N * Y * C
    ADJ, NVD = adj_ref.shape
    VT, ST = mask_ref.shape
    w = lax.axis_index("wide")
    n = lax.axis_index("narrow")
    z, y, c = w // (Y * C), (w // C) % Y, w % C
    me_r = (n * Y + y) * C + c
    me_z = z * Y + y

    def r_peer(d):
        pn = lax.rem(n + d // (Y * C), N)
        py = lax.rem(y + (d // C) % Y, Y)
        pc = lax.rem(c + d % C, C)
        return {"wide": (z * Y + py) * C + pc, "narrow": pn}, (pn * Y + py) * C + pc

    def z_peer(dz, dy):
        pz = lax.rem(z + dz, Z)
        py = lax.rem(y + dy, Y)
        return {"wide": (pz * Y + py) * C + c, "narrow": n}, pz, py

    def remote(src, dst, ssem, rsem, dev):
        return pltpu.make_async_remote_copy(
            src_ref=src, dst_ref=dst, send_sem=ssem, recv_sem=rsem,
            device_id=dev, device_id_type=MESH)

    zpairs = [(dz, dy) for dz in range(Z - 1, 0, -1) for dy in range(Y)]

    loads = [pltpu.make_async_copy(src, dst, sem_in.at[k]) for k, (src, dst) in enumerate(
        ((surf_hbm, surf_ref), (mask_hbm, mask_ref), (vol_hbm, vol_ref), (adj_hbm, adj_ref)))]
    for cp in loads:
        cp.start()

    barrier = pltpu.get_barrier_semaphore()
    for d in range(1, R):
        pl.semaphore_signal(barrier, inc=1, device_id=r_peer(d)[0], device_id_type=MESH)
    for dz, dy in zpairs:
        pl.semaphore_signal(barrier, inc=1, device_id=z_peer(dz, dy)[0], device_id_type=MESH)

    for cp in loads:
        cp.wait()
    own_xyz[...] = jnp.zeros_like(own_xyz)
    own_xyz[0:3, :] = surf_ref[...]
    vol_own[0:ADJ, :] = adj_ref[...].astype(F32)
    vol_own[ADJ:ADJ + 8, :] = jnp.zeros((8, NVD), F32)
    vol_own[ADJ:ADJ + 3, :] = vol_ref[...]
    mask_own[...] = jnp.zeros_like(mask_own)
    mask_own[:, 0:ST] = mask_ref[...].astype(F32)
    pl.semaphore_wait(barrier, R - 1 + len(zpairs))

    sends = []
    for k, (dz, dy) in enumerate(zpairs):
        dev, pz, py = z_peer(dz, dy)
        cp = remote(own_xyz, xyz_z.at[me_z], sem_xs.at[R + k], sem_xz.at[me_z], dev)
        cp.start()
        sends.append(cp)
    for d in range(1, R):
        dev, _ = r_peer(d)
        cp = remote(own_xyz, xyz_r.at[me_r], sem_xs.at[d], sem_xr.at[me_r], dev)
        cp.start()
        sends.append(cp)
    vsends = []
    if C > 1:
        dev, _ = r_peer(1)
        for k, (src, dst) in enumerate(((vol_own, vol_in), (mask_own, mask_in))):
            cp = remote(src, dst, sem_v.at[2 * k], sem_v.at[2 * k + 1], dev)
            cp.start()
            vsends.append(cp)

    expand = (lax.broadcasted_iota(jnp.int32, (VT, NVD), 1) // TILE
              == lax.broadcasted_iota(jnp.int32, (VT, NVD), 0)).astype(F32).astype(BF16)
    listed = -(-ST // 8) * 8

    def volume_features(s, vol, mask):
        adjs[s] = vol[0:ADJ, :].astype(BF16)
        f = features(vol[ADJ:ADJ + 8, :], False)
        off = ((1.0 - mask[...]) * 1024.0).T[0:listed].astype(BF16)
        pen = jnp.dot(off, expand, preferred_element_type=F32)
        rest = jnp.zeros((KP - COORD_ROWS - listed, NVD), F32)
        vfeat[s] = jnp.concatenate([f, pen, rest], axis=0).astype(BF16)

    volume_features(0, vol_own, mask_own)

    xyz_r[me_r] = own_xyz[...]
    for d in range(1, R):
        dev, s = r_peer(d)
        remote(own_xyz, xyz_r.at[s], sem_xs.at[d], sem_xr.at[s], dev).wait_recv()
    for dy in range(Y):
        py = lax.rem(y + dy, Y)
        xyz_z[z * Y + py] = xyz_r[(n * Y + py) * C + c]
    for k, (dz, dy) in enumerate(zpairs):
        dev, pz, py = z_peer(dz, dy)
        s = pz * Y + py
        remote(own_xyz, xyz_z.at[s], sem_xs.at[R + k], sem_xz.at[s], dev).wait_recv()

    extra = lax.broadcasted_iota(jnp.int32, (KP - COORD_ROWS, TILE), 0)
    for s in range(Z * Y):
        hot = jnp.where(extra == s * C + c, 1.0, 0.0)
        f = jnp.concatenate([features(xyz_z[s], True), hot], axis=0)
        sfeat[s] = f.T.astype(BF16)
    if C > 1:
        for cp in vsends:
            cp.wait_recv()
        volume_features(1, vol_in, mask_in)

    def surface_block(pz):
        left = sfeat[pl.ds(pz * Y, Y)].reshape(Y * TILE, KP)
        total = jnp.zeros((ADJ, Y * TILE), F32)
        for s in range(C):
            for k in range(0, NVD, CHUNK):
                u = jnp.dot(left, vfeat[s, :, k:k + CHUNK], preferred_element_type=F32)
                total = total + lax.dot_general(
                    adjs[s, :, k:k + CHUNK], wendland(u).astype(BF16),
                    (((1,), (1,)), ((), ())), preferred_element_type=F32)
        for q in range(Y):
            piece[pz * Y + q] = total[:, q * TILE:(q + 1) * TILE]

    def piece_copy(dz, dy):
        dev, pz, py = z_peer(dz, dy)
        s = pz * Y + py
        return remote(piece.at[s], rhs_in.at[me_z], sem_ps.at[s], sem_pr.at[me_z], dev)

    def piece_arrival(dz, dy):
        dev, pz, py = z_peer(dz, dy)
        s = pz * Y + py
        return remote(piece.at[s], rhs_in.at[s], sem_ps.at[s], sem_pr.at[s], dev), s

    def far(i, carry):
        dz = Z - 1 - i
        surface_block(lax.rem(z + dz, Z))
        for dy in range(Y):
            piece_copy(dz, dy).start()
        return carry

    lax.fori_loop(0, Z - 1, far, 0)
    surface_block(z)
    for dy in range(1, Y):
        piece_copy(0, dy).start()

    for s in range(R):
        f = jnp.concatenate(
            [features(xyz_r[s], False), jnp.zeros((KP - COORD_ROWS, TILE), F32)], axis=0)
        rfeat[:, s * TILE:(s + 1) * TILE] = f.astype(BF16)

    def kernel_rows(q, carry):
        left = sfeat[q * Y + y]
        for k in range(0, R * TILE, CHUNK):
            val = wendland(jnp.dot(left, rfeat[:, k:k + CHUNK], preferred_element_type=F32))
            high = val.astype(BF16)
            p_hi[q, :, k:k + CHUNK] = high
            p_lo[q, :, k:k + CHUNK] = (val - high.astype(F32)).astype(BF16)
        return carry

    lax.fori_loop(0, Z, kernel_rows, 0)

    rhs = piece[me_z]
    order = [(0, dy) for dy in range(1, Y)] + zpairs
    for dz, dy in order:
        cp, s = piece_arrival(dz, dy)
        cp.wait_recv()
        rhs = rhs + rhs_in[s]

    total_volume = NVD * Z * Y * C
    total_surface = TILE * Z * Y * C * N
    rhs = rhs * (RHS_GAIN / math.sqrt(total_volume) / 256.0)

    def apply_operator(o, value):
        field[o] = value
        out = []
        for dz in range(Z - 1, 0, -1):
            dev, pz, _ = z_peer(dz, 0)
            cp = remote(field.at[o], field_in.at[o, z], sem_fs.at[o, dz], sem_fr.at[o, z], dev)
            cp.start()
            out.append(cp)

        def product(f, q):
            high = f.astype(BF16)
            low = (f - high.astype(F32)).astype(BF16)
            both = jnp.dot(jnp.concatenate([high, low], axis=0), p_hi[q],
                           preferred_element_type=F32)
            return (both[0:ADJ] + both[ADJ:]
                    + jnp.dot(high, p_lo[q], preferred_element_type=F32))

        total = product(value, z)
        for dz in range(1, Z):
            dev, pz, _ = z_peer(dz, 0)
            remote(field.at[o], field_in.at[o, pz], sem_fs.at[o, dz], sem_fr.at[o, pz],
                   dev).wait_recv()
            total = total + product(field_in[o, pz], pz)
        for s in range(R):
            part[o, s] = total[:, s * TILE:(s + 1) * TILE]
        for d in range(R - 1, 0, -1):
            dev, s = r_peer(d)
            cp = remote(part.at[o, s], part_in.at[o, me_r], sem_ms.at[o, d], sem_mr.at[o, me_r],
                        dev)
            cp.start()
            out.append(cp)
        mixed = part[o, me_r]
        for d in range(1, R):
            dev, s = r_peer(d)
            remote(part.at[o, s], part_in.at[o, s], sem_ms.at[o, d], sem_mr.at[o, s],
                   dev).wait_recv()
            mixed = mixed + part_in[o, s]
        return value + (KERNEL_GAIN / total_surface / 256.0) * mixed, out

    centre = (LOWER_EDGE + UPPER_EDGE) / 2.0
    half_width = (UPPER_EDGE - LOWER_EDGE) / 2.0
    sigma = centre / half_width
    rho_zero = 1.0 / sigma
    rho_one = 1.0 / (2.0 * sigma - rho_zero)
    first = rhs / centre
    mixed, out = apply_operator(0, first)
    sends += out
    near = rhs - mixed
    update = rho_one * rho_zero * first + (2.0 * rho_one / half_width) * near
    both_ref[0] = first + update
    mixed, out = apply_operator(1, update)
    sends += out
    both_ref[1] = near - mixed

    for cp in sends + vsends:
        cp.wait_send()
    for dz, dy in order:
        piece_copy(dz, dy).wait_send()


def body(dims, vol_points, vol_adjoint, surf_points, tile_mask):
    N, Z, Y, C, KP = dims
    R = N * Y * C
    adj, nvd = vol_adjoint.shape
    vt = tile_mask.shape[0]
    vmem = pl.BlockSpec(memory_space=pltpu.VMEM)
    out = jax.ShapeDtypeStruct((2, adj, TILE), F32)
    lanes = -(-tile_mask.shape[1] // 128) * 128
    dma = pltpu.SemaphoreType.DMA
    both = pl.pallas_call(
        functools.partial(kernel, dims),
        out_shape=out,
        in_specs=[pl.BlockSpec(memory_space=pl.ANY)] * 4,
        out_specs=vmem,
        scratch_shapes=[
            pltpu.VMEM(vol_points.shape, F32),
            pltpu.VMEM(vol_adjoint.shape, BF16),
            pltpu.VMEM(surf_points.shape, F32),
            pltpu.VMEM(tile_mask.shape, jnp.int32),
            dma((4,)),
            pltpu.VMEM((8, TILE), F32),
            pltpu.VMEM((Z * Y, 8, TILE), F32),
            pltpu.VMEM((R, 8, TILE), F32),
            pltpu.VMEM((adj + 8, nvd), F32),
            pltpu.VMEM((adj + 8, nvd), F32),
            pltpu.VMEM((vt, lanes), F32),
            pltpu.VMEM((vt, lanes), F32),
            pltpu.VMEM((C, KP, nvd), BF16),
            pltpu.VMEM((C, adj, nvd), BF16),
            pltpu.VMEM((Z * Y, TILE, KP), BF16),
            pltpu.VMEM((KP, R * TILE), BF16),
            pltpu.VMEM((Z, TILE, R * TILE), BF16),
            pltpu.VMEM((Z, TILE, R * TILE), BF16),
            pltpu.VMEM((Z * Y, adj, TILE), F32),
            pltpu.VMEM((Z * Y, adj, TILE), F32),
            pltpu.VMEM((2, adj, TILE), F32),
            pltpu.VMEM((2, Z, adj, TILE), F32),
            pltpu.VMEM((2, R, adj, TILE), F32),
            pltpu.VMEM((2, R, adj, TILE), F32),
            dma((R + Z * Y,)),
            dma((Z * Y,)),
            dma((R,)),
            dma((4,)),
            dma((Z * Y,)),
            dma((Z * Y,)),
            dma((2, Z)),
            dma((2, Z)),
            dma((2, R)),
            dma((2, R)),
        ],
        compiler_params=pltpu.CompilerParams(
            collective_id=0, has_side_effects=True, vmem_limit_bytes=56 * 1024 * 1024),
    )(vol_points, vol_adjoint, surf_points, tile_mask)
    return both[0], both[1]


def solution(mesh):
    wide, narrow = mesh.shape["wide"], mesh.shape["narrow"]
    core = math.gcd(wide, 2)
    rows = math.gcd(wide // core, 2)
    depth = -(-(COORD_ROWS + wide) // 128) * 128
    dims = (narrow, wide // core // rows, rows, core, depth)
    return jax.shard_map(
        functools.partial(body, dims),
        mesh=mesh,
        in_specs=(
            P(None, "wide"),
            P(None, "wide"),
            P(None, ("narrow", "wide")),
            P("wide", "narrow"),
        ),
        out_specs=(P(None, ("narrow", "wide")), P(None, ("narrow", "wide"))),
        check_vma=False,
    )
```
